256 devices in a mesh: mat: 16 (over z, core), pts: 16 (over y, x).
Axes of the slice: x: 4, y: 4, z: 8, core: 2. Of those that a mesh axis runs over, the one named last changes fastest.
Arguments:
- dens_blocks: bfloat16 [16, 2048, 2048], P(None, 'pts', 'mat'), may hold values from -0.00390625 to 0.00390625
- basis_values: bfloat16 [16, 24576, 1536], P('mat', 'pts'), may hold values from -6 to 6
- kernel: float32 [16, 24576], P('mat', 'pts'), may hold values from 0.3 to 3
- perturbation: float32 [16, 24576], P('mat', 'pts'), may hold values from -6 to 6
- quad_weight: float32 [16, 24576], P('mat', 'pts'), may hold values from 0.002 to 0.02
- point_count: int32 [16, 16], P('mat', 'pts'), may hold values from 192 to 1536, as said below
- active_blocks: int32 [16, 16, 12], P('mat', 'pts'), may hold values from 0 to 15, as said below
- block_pattern: int32 [16, 16, 16], replicated, may hold values 0 or 1
Outputs:
- h_response: float32 [16, 2048, 2048], P(None, 'pts', 'mat')
- n_response: float32 [16, 24576], P('mat', 'pts')
The draws below stay inside these ranges and needn't reach their ends.
Inputs may be any that keep to these rules, and one draw needn't show every extreme that they name: `point_count`: each cluster has at least one shard with exactly 1536 points in use; the others hold 192 or more. `active_blocks`: the 12 entries of one shard are distinct block numbers of its cluster, in no particular order.
All inputs are finite; a program needn't handle non-finite values.
Results may differ from the reference program's by a relative error of at most 0.011.
Values may be sent and summed in bfloat16 or wider, within the bound.
A program may use at most 128 MiB of HBM per device.

```python
import math
import jax
import jax.numpy as jnp
from jax import lax

BLOCK = 128
ACT = 16
NACT = 12
PTS = 1536
ORB = 2048
NCL = 16
NSHARD = 16
NPTS = 24576


def draw_point_count(key, part):
    key_low = jax.random.fold_in(key, 11)
    key_full = jax.random.fold_in(key, 12)
    counts = jax.random.randint(key_low, (NCL, NSHARD), PTS // 8, PTS + 1, dtype=jnp.int32)
    full_shard = jax.random.randint(key_full, (NCL,), 0, NSHARD, dtype=jnp.int32)
    column = jnp.arange(NSHARD, dtype=jnp.int32)
    return jnp.where(column[None, :] == full_shard[:, None], PTS, counts).astype(jnp.int32)


def draw_active_blocks(key, part):
    subkeys = jax.random.split(jax.random.fold_in(key, 21), NCL * NSHARD)
    orders = jax.vmap(lambda subkey: jax.random.permutation(subkey, ACT))(subkeys)
    return orders[:, :NACT].reshape(NCL, NSHARD, NACT).astype(jnp.int32)


def plant(drawn, key, smallest, top_value):
    place = [jax.random.randint(jax.random.fold_in(key, axis), (), 0, length) for axis, length in enumerate(drawn.shape)]
    longest = drawn.shape.index(max(drawn.shape))
    next_to = place[:longest] + [(place[longest] + 1) % drawn.shape[longest]] + place[longest + 1:]
    return drawn.at[tuple(place)].set(smallest).at[tuple(next_to)].set(top_value)


def shard_levels(own_key, shape, pieces, low, largest):
    loudness, own = 1.0, jax.random.fold_in(own_key, 6)
    for position, blocks in pieces:
        steps = jnp.exp(jax.random.uniform(jax.random.fold_in(own, position), (blocks,), jnp.float32, low / len(pieces), largest / len(pieces)))
        loudness = loudness * jnp.repeat(steps, shape[position] // blocks).reshape([-1 if axis == position else 1 for axis in range(len(shape))])
    return loudness


def scatter_about(stream_key, extent, deviation, most, pieces=(), kind=jnp.bfloat16):
    level = shard_levels(stream_key, extent, pieces, -0.22, 0.18) if pieces else 1.0
    drawn = jax.random.normal(stream_key, extent, jnp.float32) * deviation * level
    return jnp.minimum(jnp.maximum(drawn, -most), most).astype(kind)


def setup_inputs(seed: int = 0) -> dict:
    key_of = jax.random.split(jax.random.key(seed), 9)
    return {
        "dens_blocks": scatter_about(key_of[0], (NCL, ORB, ORB), (NACT * NACT * BLOCK * BLOCK) ** -0.5, 0.00390625, ((1, 16), (2, 16))),
        "basis_values": scatter_about(key_of[1], (NCL, NPTS, NACT * BLOCK), 1.0, 6.0, ((0, 16), (1, 16))),
        "kernel": jnp.clip(jnp.exp(math.log(3.0) - 2.3025851 * jax.random.uniform(key_of[2], (NCL, NPTS), jnp.float32) ** shard_levels(key_of[2], (NCL, NPTS), ((0, 16), (1, 16)), -0.2, 0.2)), 0.3, 3.0),
        "perturbation": scatter_about(key_of[3], (NCL, NPTS), 1.0, 6.0, ((0, 16), (1, 16)), jnp.float32),
        "quad_weight": jnp.clip(jnp.exp(math.log(0.02) - 2.30258502 * jax.random.uniform(key_of[4], (NCL, NPTS), jnp.float32) ** shard_levels(key_of[4], (NCL, NPTS), ((0, 16), (1, 16)), -0.2, 0.2)), 0.002, 0.02),
        "point_count": draw_point_count(jax.random.fold_in(key_of[8], 71), 0),
        "active_blocks": draw_active_blocks(jax.random.fold_in(key_of[8], 71), 0),
        "block_pattern": plant((jax.random.randint(key_of[7], (NCL, ACT, ACT), 0, 4) < 3).astype(jnp.int32), jax.random.fold_in(key_of[7], 1), 0, 1),
    }


def point_block(basis_rows, kernel_rows, perturb_rows, weight_rows, first_point, point_total, submatrix):
    row_count = basis_rows.shape[0]
    inside = (first_point + jnp.arange(row_count, dtype=jnp.int32)) < point_total
    product = jnp.dot(basis_rows, submatrix, preferred_element_type=jnp.float32)
    density = jnp.where(inside, jnp.sum(product * basis_rows.astype(jnp.float32), axis=1), 0.0)
    scaling = jnp.where(inside, weight_rows * (perturb_rows - kernel_rows * density), 0.0)
    scaled = (scaling[:, None] * basis_rows.astype(jnp.float32)).astype(jnp.bfloat16)
    partial_h = jnp.dot(basis_rows.T, scaled, preferred_element_type=jnp.float32)
    return density, partial_h


def reference(dens_blocks, basis_values, kernel, perturbation, quad_weight, point_count, active_blocks, block_pattern):
    def cluster_terms(cluster):
        cluster_density = dens_blocks[cluster]
        cluster_pattern = block_pattern[cluster]
        masked = cluster_density.reshape(ACT, BLOCK, ACT, BLOCK) * cluster_pattern.astype(jnp.bfloat16)[:, None, :, None]

        def shard_step(h_total, shard_id):
            chosen = active_blocks[cluster, shard_id]
            submatrix = masked[chosen][:, :, chosen].reshape(NACT * BLOCK, NACT * BLOCK)
            first_row = shard_id * PTS
            basis_rows = lax.dynamic_slice_in_dim(basis_values[cluster], first_row, PTS, 0)
            kernel_rows = lax.dynamic_slice_in_dim(kernel[cluster], first_row, PTS, 0)
            perturb_rows = lax.dynamic_slice_in_dim(perturbation[cluster], first_row, PTS, 0)
            weight_rows = lax.dynamic_slice_in_dim(quad_weight[cluster], first_row, PTS, 0)
            density, partial_h = point_block(basis_rows, kernel_rows, perturb_rows, weight_rows, 0, point_count[cluster, shard_id], submatrix)
            rounded = lax.optimization_barrier(partial_h.astype(jnp.bfloat16))
            packed = rounded.astype(jnp.float32).reshape(NACT, BLOCK, NACT, BLOCK).transpose(0, 2, 1, 3)
            spread = jnp.zeros((ACT, ACT, BLOCK, BLOCK), jnp.float32).at[chosen[:, None], chosen[None, :]].set(packed)
            return h_total + spread, density

        h_total, densities = lax.scan(shard_step, jnp.zeros((ACT, ACT, BLOCK, BLOCK), jnp.float32), jnp.arange(NSHARD, dtype=jnp.int32))
        mask_full = jnp.repeat(jnp.repeat(cluster_pattern.astype(jnp.float32), BLOCK, axis=0), BLOCK, axis=1)
        h_cluster = h_total.transpose(0, 2, 1, 3).reshape(ORB, ORB) * mask_full
        return h_cluster, densities.reshape(NPTS)

    h_all, n_all = lax.map(cluster_terms, jnp.arange(NCL, dtype=jnp.int32))
    return h_all, n_all
```

```python
import jax
import jax.numpy as jnp
from jax import lax
from jax.experimental import pallas as pl
from jax.experimental.pallas import tpu as pltpu
from jax.sharding import PartitionSpec as P

NB = 16
SIDE = 4
NOWN = 9
MESH = pl.DeviceIdType.MESH
F32 = jnp.float32
BF16 = jnp.bfloat16


def _kernel(
    dens, basis, kern, pert, weight, count, active, pattern,
    h_out, n_out,
    first, packed, rows_x, cols_x, gath, zacc, scal, col3, scaled, hpart,
    relay_in, plus_in, minus_in, relay2_in, plus2_in, minus2_in,
    final, flipped, back,
    basis_sem, a_send, a_recv, g_send, g_recv, s_send, s_recv, d_send, d_recv,
):
    blk = dens.shape[1]
    nact, pts = packed.shape[0], packed.shape[1]
    quarter = NOWN * blk // 4
    wide = (NOWN + 1) * blk
    m = lax.axis_index("mat")
    s = lax.axis_index("pts")
    x = lax.rem(s, SIDE)
    y = lax.div(s, SIDE)

    def md(v, n):
        return lax.rem(v + n, n)

    def near(axis, step):
        if axis == 0:
            return (m, y * SIDE + md(x + step, SIDE))
        return (m, md(y + step, SIDE) * SIDE + x)

    def al(v, k):
        return pl.multiple_of(v, k)

    def chunk(ref, t, k):
        r = lax.rem(t, 2)
        return ref.at[
            lax.div(t, 2),
            pl.ds(al(r * blk + k * quarter, 16), quarter),
            pl.ds(al(r * blk, blk), blk),
        ]

    def remote(src, dst, ssem, rsem, dev):
        return pltpu.make_async_remote_copy(
            src_ref=src, dst_ref=dst, send_sem=ssem, recv_sem=rsem,
            device_id=dev, device_id_type=MESH,
        )

    sends = []

    def send(src, dst, ssem, rsem, dev):
        cp = remote(src, dst, ssem, rsem, dev)
        cp.start()
        sends.append(cp)

    def landed(dst, ssem, rsem):
        remote(dst, dst, ssem, rsem, (m, s)).wait_recv()

    loads = [
        pltpu.make_async_copy(basis.at[:, pl.ds(j * blk, blk)], packed.at[j], basis_sem.at[j])
        for j in range(packed.shape[0])
    ]
    for cp in loads:
        cp.start()
    diff = md(m - s, NB)
    own = diff < NB // 2
    other = jnp.where(own, s, m)

    barrier = pltpu.get_barrier_semaphore()
    for d in range(NB // 2):
        src = lax.rem(s + d, NB)

        @pl.when(src != m)
        def _():
            pl.semaphore_signal(barrier, inc=1, device_id=(src, s), device_id_type=MESH)

    for d in range(1, NOWN):
        pl.semaphore_signal(
            barrier, inc=1, device_id=(s, lax.rem(s + d, NB)), device_id_type=MESH
        )
    for axis in (0, 1):
        for step in (1, -1):
            pl.semaphore_signal(barrier, inc=1, device_id=near(axis, step), device_id_type=MESH)
    pl.semaphore_wait(barrier, NB + 4 - own.astype(jnp.int32))

    slot = jnp.where(own, diff, NB + NB // 2 - 1 - diff)

    def first_copy(k):
        c = lax.rem(m + k, NB)
        return remote(dens.at[c], first.at[slot], a_send.at[k], a_recv.at[slot], (c, other))

    for k in (8, 7, 9, 6, 10, 5, 11, 4, 12, 3, 13, 2, 14, 1, 15):
        first_copy(k).start()

    @pl.when(jnp.logical_not(own))
    def _():
        first_copy(0).start()

    @pl.when(own)
    def _():
        first[diff] = dens[m]

    zacc[...] = jnp.zeros_like(zacc)
    for q in range(NB // 2):
        gath[q, pl.ds(NOWN * blk, blk), pl.ds(0, blk)] = jnp.zeros((blk, blk), BF16)
        gath[q, pl.ds(0, blk), pl.ds(blk, blk)] = jnp.zeros((blk, blk), BF16)
    for i in range(pts // blk):
        at = pl.ds(i * blk, blk)
        for j, ref in enumerate((kern, pert, weight)):
            col3[j, at, :] = jnp.broadcast_to(ref[0:1, at], (blk, blk)).T
    for cp in loads:
        cp.wait()
    part = pts // 3

    def spread(a, carry):
        pos = jnp.int32(0)
        hits = jnp.int32(0)
        for j in range(nact):
            hit = (active[0, j] == a).astype(jnp.int32)
            pos = pos + j * hit
            hits = hits + hit
        pos = jnp.minimum(pos, nact - 1)
        for i in range(3):
            at = pl.ds(i * part, part)
            v = packed[pos, at, :]
            v = jnp.where(hits > 0, v, jnp.zeros_like(v))
            vt = v.T
            rows_x[at, pl.ds(al(a * blk, blk), blk)] = v
            cols_x[pl.ds(al(a * blk, blk), blk), at] = vt

            @pl.when(a < NB // 2)
            def _():
                rows_x[at, pl.ds(al((a + NB) * blk, blk), blk)] = v
                cols_x[pl.ds(al((a + NB) * blk, blk), blk), at] = vt

        return carry

    lax.fori_loop(0, NB, spread, 0)

    def first_landed(j):
        landed(first.at[j], a_send.at[0], a_recv.at[j])

    def pat(a, b):
        return pattern[m, a, b].astype(F32)

    r = lax.rem(s, 2)
    mine = lax.div(s, 2)
    for d in range(NOWN):
        sd = lax.rem(s + d, NB)
        if d < NB // 2:

            @pl.when(sd != m)
            def _():
                first_landed(d)

        if d >= 1:
            first_landed(NB // 2 - 1 + d)
        if d == 0:
            v = first[0].astype(F32) * pat(s, s)
        else:
            v = first[NB // 2 - 1 + d].astype(F32) * pat(sd, s)
            if d < NB // 2:
                v = v + (first[d].astype(F32) * pat(s, sd)).T
        gath[mine, pl.ds(al((r + d) * blk, blk), blk), pl.ds(al(r * blk, blk), blk)] = v.astype(BF16)

    def axes(k):
        return (0, 1) if k < 2 else (1, 0)

    def sign(k):
        return 1 if k % 2 == 0 else -1

    def shard(k, du, dv):
        dx, dy = (du, dv) if k < 2 else (dv, du)
        return md(y + dy, SIDE) * SIDE + md(x + dx, SIDE)

    def gsem(k, du, dv):
        return k * 16 + (du % SIDE) * SIDE + dv % SIDE

    def g_put(k, du, dv, stage, step):
        ref = chunk(gath, shard(k, du, dv), k)
        idx = gsem(k, du - step, dv) if stage == 0 else gsem(k, du, dv - step)
        send(ref, ref, g_send.at[idx], g_recv.at[idx], near(axes(k)[stage], step))

    def g_get(k, du, dv):
        idx = gsem(k, du, dv)
        landed(chunk(gath, shard(k, du, dv), k), g_send.at[idx], g_recv.at[idx])

    def g_on(k, du, dv):
        if dv % SIDE == 0:
            if du % SIDE == (-sign(k)) % SIDE:
                g_put(k, du, dv, 0, sign(k))
            g_put(k, du, dv, 1, 1)
            g_put(k, du, dv, 1, -1)
        elif dv % SIDE == (-sign(k)) % SIDE:
            g_put(k, du, dv, 1, sign(k))

    mt = pts // 3

    def density_pair(q):
        lane = q * 2 * blk

        def step(i, carry):
            at = pl.ds(al(i * mt, mt), mt)
            prod = jnp.dot(
                rows_x[at, pl.ds(al(lane, blk), wide)], gath[q], preferred_element_type=F32
            )
            prod = prod * rows_x[at, pl.ds(al(lane, blk), 2 * blk)].astype(F32)
            zacc[at, :] += prod[:, :blk] + prod[:, blk:]
            return carry

        lax.fori_loop(0, 3, step, 0)

    xpair = lax.div(x, 2)

    def pair_at(far, dy):
        xp = 1 - xpair if far else xpair
        return md(y + dy, SIDE) * (SIDE // 2) + xp

    quarters = range(4)
    for k in quarters:
        g_put(k, 0, 0, 0, 1)
        g_put(k, 0, 0, 0, -1)
    for k in quarters:
        g_put(k, 0, 0, 1, 1)
        g_put(k, 0, 0, 1, -1)

    def take(offsets):
        for du, dv in offsets:
            for k in quarters:
                g_get(k, du * sign(k), dv * sign(k))
                g_on(k, du * sign(k), dv * sign(k))

    take([(-1, 0), (0, -1), (1, 0), (0, 1)])
    density_pair(pair_at(False, 0))
    take([(2, 0), (-1, -1), (1, -1), (-1, 1), (1, 1)])
    density_pair(pair_at(False, 1))
    take([(2, -1), (0, 2)])
    density_pair(pair_at(False, -1))
    take([(2, 1)])
    density_pair(pair_at(True, 0))
    take([(-1, 2), (1, 2)])
    density_pair(pair_at(True, 1))
    density_pair(pair_at(True, -1))
    density_pair(pair_at(False, 2))
    take([(2, 2)])
    density_pair(pair_at(True, 2))

    total = count[0, 0]
    for i in range(pts // blk):
        at = pl.ds(i * blk, blk)
        dens_col = jnp.broadcast_to(jnp.sum(zacc[at, :], axis=1, keepdims=True), (blk, blk))
        inside = lax.broadcasted_iota(jnp.int32, (blk, blk), 0) + i * blk < total
        dens_col = jnp.where(inside, dens_col, 0.0)
        zacc[at, :] = dens_col
        scal[at, :] = jnp.where(
            inside, col3[2, at, :] * (col3[1, at, :] - col3[0, at, :] * dens_col), 0.0
        )

    def partial_pair(q):
        lane = q * 2 * blk

        def scale(i, carry):
            at = pl.ds(al(i * blk, blk), blk)
            f = scal[at, :]
            v = rows_x[at, pl.ds(al(lane, blk), 2 * blk)].astype(F32)
            scaled[at, :] = jnp.concatenate([v[:, :blk] * f, v[:, blk:] * f], axis=1).astype(BF16)
            return carry

        lax.fori_loop(0, pts // blk, scale, 0, unroll=2)
        half = wide // 2

        def step(i, carry):
            o = pl.ds(al(lane + i * half, blk), half)
            v = jnp.dot(cols_x[o, :], scaled[...], preferred_element_type=F32)
            hpart[q, pl.ds(al(i * half, blk), half), :] = v.astype(BF16)
            return carry

        lax.fori_loop(0, 2, step, 0)

    def s_axes(k):
        return (1, 0) if k < 2 else (0, 1)

    def s_shard(k, du, j):
        if k < 2:
            return md(y + du, SIDE) * SIDE + j
        return j * SIDE + md(x + du, SIDE)

    def add_into(ref, *others):
        v = ref[...].astype(F32)
        for o in others:
            v = v + o[...].astype(F32)
        ref[...] = v.astype(BF16)

    def h_far(k, j):
        ref = chunk(hpart, s_shard(k, 2, j), k)
        i = k * SIDE + j
        send(ref, relay_in.at[k, j], s_send.at[i], s_recv.at[i], near(s_axes(k)[0], sign(k)))

    def h_direct(k, j):
        ref = chunk(hpart, s_shard(k, -sign(k), j), k)
        i = k * SIDE + j
        send(ref, minus_in.at[k, j], s_send.at[16 + i], s_recv.at[16 + i], near(s_axes(k)[0], -sign(k)))

    def h_relay(k, j):
        ref = chunk(hpart, s_shard(k, sign(k), j), k)
        i = k * SIDE + j
        landed(relay_in.at[k, j], s_send.at[i], s_recv.at[i])
        add_into(ref, relay_in.at[k, j])
        send(ref, plus_in.at[k, j], s_send.at[32 + i], s_recv.at[32 + i], near(s_axes(k)[0], sign(k)))

    def h_sum(k, j):
        ref = chunk(hpart, s_shard(k, 0, j), k)
        i = k * SIDE + j
        landed(plus_in.at[k, j], s_send.at[32 + i], s_recv.at[32 + i])
        landed(minus_in.at[k, j], s_send.at[16 + i], s_recv.at[16 + i])
        add_into(ref, plus_in.at[k, j], minus_in.at[k, j])

    def v_at(k, dv):
        return md((x if k < 2 else y) + dv, SIDE)

    def h2_far(k):
        ref = chunk(hpart, s_shard(k, 0, v_at(k, 2)), k)
        send(ref, relay2_in.at[k], s_send.at[48 + k], s_recv.at[48 + k], near(s_axes(k)[1], sign(k)))

    def h2_direct(k):
        ref = chunk(hpart, s_shard(k, 0, v_at(k, -sign(k))), k)
        send(ref, minus2_in.at[k], s_send.at[52 + k], s_recv.at[52 + k], near(s_axes(k)[1], -sign(k)))

    def h2_relay(k):
        ref = chunk(hpart, s_shard(k, 0, v_at(k, sign(k))), k)
        landed(relay2_in.at[k], s_send.at[48 + k], s_recv.at[48 + k])
        add_into(ref, relay2_in.at[k])
        send(ref, plus2_in.at[k], s_send.at[56 + k], s_recv.at[56 + k], near(s_axes(k)[1], sign(k)))

    def h2_sum(k):
        ref = chunk(hpart, s_shard(k, 0, v_at(k, 0)), k)
        landed(plus2_in.at[k], s_send.at[56 + k], s_recv.at[56 + k])
        landed(minus2_in.at[k], s_send.at[52 + k], s_recv.at[52 + k])
        v = ref[...].astype(F32) + plus2_in[k].astype(F32) + minus2_in[k].astype(F32)
        final[pl.ds(k * quarter, quarter), :] = v.astype(BF16)

    late = []
    for dy in (2, 1, -1, 0):
        for far in (True, False):
            partial_pair(pair_at(far, dy))
            due, late = late, []
            xp = 1 - xpair if far else xpair
            ky = v_at(2, dy)
            js = [xp * 2, xp * 2 + 1]
            if dy == 2:
                for j in js:
                    h_far(0, j)
                    h_far(1, j)
            elif dy != 0:
                k_direct, k_relay = (1, 0) if dy == 1 else (0, 1)
                for j in js:
                    h_direct(k_direct, j)
                    late.append((k_relay, j))
            if far:
                h_far(2, ky)
                h_far(3, ky)
            else:
                h_direct(3, ky)
                h_direct(2, ky)
                late.append((2, ky))
                late.append((3, ky))
            for k, j in due:
                h_relay(k, j)
    for k, j in late:
        h_relay(k, j)

    for i in range(pts // blk):
        at = pl.ds(i * blk, blk)
        n_out[0:1, at] = zacc[at, :].T[0:1, :]

    for k in quarters:
        h_sum(k, v_at(k, 2))
        h2_far(k)
    for k in quarters:
        h_sum(k, v_at(k, -sign(k)))
        h2_direct(k)
    for k in quarters:
        h_sum(k, v_at(k, sign(k)))
        h2_relay(k)
    for k in quarters:
        h_sum(k, v_at(k, 0))
    for k in quarters:
        h2_sum(k)

    def d_direct(d):
        return remote(
            final.at[pl.ds(d * blk, blk)], back.at[m], d_send.at[d], d_recv.at[m],
            (s, lax.rem(s + d, NB)),
        )

    def d_flip(d):
        return remote(
            flipped.at[d], back.at[m], d_send.at[NOWN + d - 1], d_recv.at[m],
            (lax.rem(s + d, NB), s),
        )

    for d in range(NOWN):
        if d == 0:

            @pl.when(m != s)
            def _():
                d_direct(0).start()

            @pl.when(m == s)
            def _():
                back[m] = final[pl.ds(0, blk), :]
        else:
            d_direct(d).start()
    for d in range(1, NB // 2):
        flipped[d] = final[pl.ds(d * blk, blk), :].astype(F32).T.astype(BF16)
        sd = lax.rem(s + d, NB)

        @pl.when(m != sd)
        def _():
            d_flip(d).start()

        @pl.when(m == sd)
        def _():
            back[m] = flipped[d]

    for k in range(1, NB):
        first_copy(k).wait_send()

    @pl.when(jnp.logical_not(own))
    def _():
        first_copy(0).wait_send()

    for cp in sends:
        cp.wait_send()

    for k in (15, 1, 14, 2, 13, 3, 12, 4, 11, 5, 10, 6, 9, 7, 8, 0):
        c = lax.rem(m + k, NB)

        def got():
            landed(back.at[c], d_send.at[0], d_recv.at[c])

        if k == 0:
            pl.when(jnp.logical_not(own))(got)
        else:
            got()
        h_out[c] = back[c].astype(F32) * pattern[c, s, m].astype(F32)

    for d in range(NOWN):
        if d == 0:

            @pl.when(m != s)
            def _():
                d_direct(0).wait_send()
        else:
            d_direct(d).wait_send()
    for d in range(1, NB // 2):

        @pl.when(m != lax.rem(s + d, NB))
        def _():
            d_flip(d).wait_send()


def body(dens, basis, kern, pert, weight, count, active, pattern):
    blk = dens.shape[1]
    pts = basis.shape[1]
    nact = basis.shape[2] // blk
    quarter = NOWN * blk // 4
    wide = (NOWN + 1) * blk
    ext = NB + NB // 2
    vmem = pl.BlockSpec(memory_space=pltpu.VMEM)
    smem = pl.BlockSpec(memory_space=pltpu.SMEM)
    dma = pltpu.SemaphoreType.DMA
    return pl.pallas_call(
        _kernel,
        out_shape=(
            jax.ShapeDtypeStruct((NB, blk, blk), F32),
            jax.ShapeDtypeStruct((1, pts), F32),
        ),
        in_specs=[vmem, pl.BlockSpec(memory_space=pl.ANY), vmem, vmem, vmem, smem, smem, smem],
        out_specs=(vmem, vmem),
        scratch_shapes=[
            pltpu.VMEM((NB, blk, blk), BF16),
            pltpu.VMEM((nact, pts, blk), BF16),
            pltpu.VMEM((pts, ext * blk), BF16),
            pltpu.VMEM((ext * blk, pts), BF16),
            pltpu.VMEM((NB // 2, wide, 2 * blk), BF16),
            pltpu.VMEM((pts, blk), F32),
            pltpu.VMEM((pts, blk), F32),
            pltpu.VMEM((3, pts, blk), F32),
            pltpu.VMEM((pts, 2 * blk), BF16),
            pltpu.VMEM((NB // 2, wide, 2 * blk), BF16),
            pltpu.VMEM((4, SIDE, quarter, blk), BF16),
            pltpu.VMEM((4, SIDE, quarter, blk), BF16),
            pltpu.VMEM((4, SIDE, quarter, blk), BF16),
            pltpu.VMEM((4, quarter, blk), BF16),
            pltpu.VMEM((4, quarter, blk), BF16),
            pltpu.VMEM((4, quarter, blk), BF16),
            pltpu.VMEM((NOWN * blk, blk), BF16),
            pltpu.VMEM((NB // 2, blk, blk), BF16),
            pltpu.VMEM((NB, blk, blk), BF16),
            dma((nact,)), dma((16,)), dma((16,)), dma((64,)), dma((64,)),
            dma((60,)), dma((60,)), dma((16,)), dma((16,)),
        ],
        compiler_params=pltpu.CompilerParams(
            collective_id=0, has_side_effects=True, vmem_limit_bytes=60 * 1024 * 1024
        ),
    )(
        dens, basis.reshape(basis.shape[1:]), kern, pert, weight, count,
        active.reshape(1, active.shape[-1]), pattern,
    )


def solution(mesh):
    placed = (
        P(None, "pts", "mat"),
        P("mat", "pts", None),
        P("mat", "pts"),
        P("mat", "pts"),
        P("mat", "pts"),
        P("mat", "pts"),
        P("mat", "pts", None),
        P(),
    )
    return jax.shard_map(
        body,
        mesh=mesh,
        in_specs=placed,
        out_specs=(P(None, "pts", "mat"), P("mat", "pts")),
        check_vma=False,
    )
```

```python
import jax
import jax.numpy as jnp
from jax import lax
from jax.experimental import pallas as pl
from jax.experimental.pallas import tpu as pltpu
from jax.sharding import PartitionSpec as P

NB = 16
SIDE = 4
NOWN = 9
MESH = pl.DeviceIdType.MESH
F32 = jnp.float32
BF16 = jnp.bfloat16


STAGE_BLOCKS = (5, 4)
HALF_EXT = 12
LEVELS = (
    ((-1, 0), (0, -1), (1, 0), (0, 1)),
    ((2, 0), (-1, -1), (1, -1), (-1, 1), (1, 1)),
    ((2, -1), (0, 2), (2, 1), (-1, 2), (1, 2)),
    ((2, 2),),
)


def _kernel(
    dens, basis, kern, pert, weight, count, active, pattern,
    h_out, n_out,
    first, packed, rows_x, cols_x, gath0, gath1, zacc, scal, col3, scaled, hpart0, hpart1,
    relay_in, plus_in, minus_in, relay2_in, plus2_in, minus2_in,
    final, flipped, mid, back,
    basis_sem, a_send, a_recv, g_send, g_recv, s_send, s_recv,
    m_send, m_recv, d_send, d_recv,
):
    blk = dens.shape[1]
    nact, pts = packed.shape[0], packed.shape[1]
    gath = (gath0, gath1)
    hpart = (hpart0, hpart1)
    stage_rows = [n * blk for n in STAGE_BLOCKS]
    half = [n // 2 for n in stage_rows]
    wide = [n + blk for n in stage_rows]
    m = lax.axis_index("mat")
    s = lax.axis_index("pts")
    x = lax.rem(s, SIDE)
    y = lax.div(s, SIDE)

    def md(v, n):
        return lax.rem(v + 2 * n, n)

    def partner(t, d):
        return lax.rem(t + d + NB // 2 * (d % 2), NB)

    def al(v, k):
        return pl.multiple_of(v, k)

    def near(axis, step):
        if axis == 0:
            return (m, y * SIDE + md(x + step, SIDE))
        return (m, md(y + step, SIDE) * SIDE + x)

    quarters = range(4)

    def sign(k):
        return 1 if k < 2 else -1

    def chunk(bufs, xx, yy, k):
        r = lax.div(xx, 2)
        return bufs[k // 2].at[
            yy * 2 + lax.rem(xx, 2),
            pl.ds(al(r * blk + (k % 2) * half[k // 2], 16), half[k // 2]),
            pl.ds(al(r * blk, blk), blk),
        ]

    def remote(src, dst, ssem, rsem, dev):
        return pltpu.make_async_remote_copy(
            src_ref=src, dst_ref=dst, send_sem=ssem, recv_sem=rsem,
            device_id=dev, device_id_type=MESH,
        )

    sends = []

    def send(src, dst, ssem, rsem, dev):
        cp = remote(src, dst, ssem, rsem, dev)
        cp.start()
        sends.append(cp)

    def landed(dst, ssem, rsem):
        remote(dst, dst, ssem, rsem, (m, s)).wait_recv()

    loads = [
        pltpu.make_async_copy(basis.at[:, pl.ds(j * blk, blk)], packed.at[j], basis_sem.at[j])
        for j in range(nact)
    ]
    for cp in loads:
        cp.start()
    diff = md(m - s, NB)
    diff = lax.rem(diff + NB // 2 * lax.rem(diff, 2), NB)
    own = diff < NB // 2
    other = jnp.where(own, s, m)

    barrier = pltpu.get_barrier_semaphore()
    for d in range(NB // 2):
        src = partner(s, d)

        @pl.when(src != m)
        def _():
            pl.semaphore_signal(barrier, inc=1, device_id=(src, s), device_id_type=MESH)

    for d in range(1, NOWN):
        pl.semaphore_signal(
            barrier, inc=1, device_id=(s, partner(s, d)), device_id_type=MESH
        )
    for axis in (0, 1):
        for step in (1, -1):
            pl.semaphore_signal(barrier, inc=1, device_id=near(axis, step), device_id_type=MESH)
    pl.semaphore_wait(barrier, NB + 4 - own.astype(jnp.int32))

    slot = jnp.where(own, diff, NB + NB // 2 - 1 - diff)

    def first_copy(k):
        c = lax.rem(m + k, NB)
        return remote(dens.at[c], first.at[slot], a_send.at[k], a_recv.at[slot], (c, other))

    def first_sends():
        for k in (8, 7, 9, 6, 10, 5, 11, 4, 12, 3, 13, 2, 14, 1, 15):
            first_copy(k).start()

        @pl.when(jnp.logical_not(own))
        def _():
            first_copy(0).start()

        @pl.when(own)
        def _():
            first[diff] = dens[m]

    first_sends()

    zacc[...] = jnp.zeros_like(zacc)
    for st in (0, 1):
        for q in range(NB // 2):
            gath[st][q, pl.ds(stage_rows[st], blk), pl.ds(0, blk)] = jnp.zeros((blk, blk), BF16)
            gath[st][q, pl.ds(0, blk), pl.ds(blk, blk)] = jnp.zeros((blk, blk), BF16)
    for i in range(pts // blk):
        at = pl.ds(i * blk, blk)
        for j, ref in enumerate((kern, pert, weight)):
            col3[j, at, :] = jnp.broadcast_to(ref[0:1, at], (blk, blk)).T
    for cp in loads:
        cp.wait()
    part = pts // 3

    def spread(a, carry):
        pos = jnp.int32(0)
        hits = jnp.int32(0)
        for j in range(nact):
            hit = (active[0, j] == a).astype(jnp.int32)
            pos = pos + j * hit
            hits = hits + hit
        pos = jnp.minimum(pos, nact - 1)
        lead = lax.div(a, 2)
        to = lax.rem(a, 2) * HALF_EXT + lead
        for i in range(3):
            at = pl.ds(i * part, part)
            v = packed[pos, at, :]
            v = jnp.where(hits > 0, v, jnp.zeros_like(v))
            vt = v.T
            rows_x[at, pl.ds(al(to * blk, blk), blk)] = v
            cols_x[pl.ds(al(to * blk, blk), blk), at] = vt

            @pl.when(lead < HALF_EXT - NB // 2)
            def _():
                again = to + NB // 2
                rows_x[at, pl.ds(al(again * blk, blk), blk)] = v
                cols_x[pl.ds(al(again * blk, blk), blk), at] = vt

        return carry

    lax.fori_loop(0, NB, spread, 0)

    def first_landed(j):
        landed(first.at[j], a_send.at[0], a_recv.at[j])

    def pat(a, b):
        return pattern[m, a, b].astype(F32)

    r_own = lax.div(x, 2)
    q_own = y * 2 + lax.rem(x, 2)

    def pair_sums(st):
        for d in range(st, NOWN, 2):
            sd = partner(s, d)
            if d < NB // 2:

                @pl.when(sd != m)
                def _():
                    first_landed(d)

            if d >= 1:
                first_landed(NB // 2 - 1 + d)
            if d == 0:
                v = first[0].astype(F32) * pat(s, s)
            else:
                v = first[NB // 2 - 1 + d].astype(F32) * pat(sd, s)
                if d < NB // 2:
                    v = v + (first[d].astype(F32) * pat(s, sd)).T
            gath[st][
                q_own, pl.ds(al((r_own + d // 2) * blk, blk), blk), pl.ds(al(r_own * blk, blk), blk)
            ] = v.astype(BF16)

    def g_axes(k):
        return (0, 1) if k % 2 == 0 else (1, 0)

    def g_chunk(k, du, dv):
        dx, dy = (du, dv) if k % 2 == 0 else (dv, du)
        return chunk(gath, md(x + dx, SIDE), md(y + dy, SIDE), k)

    def gsem(k, du, dv):
        return k * 16 + (du % SIDE) * SIDE + dv % SIDE

    def g_put(k, du, dv, hop, step):
        ref = g_chunk(k, du, dv)
        idx = gsem(k, du - step, dv) if hop == 0 else gsem(k, du, dv - step)
        send(ref, ref, g_send.at[idx], g_recv.at[idx], near(g_axes(k)[hop], step))

    def g_start(st):
        for hop in (0, 1):
            for k in (2 * st, 2 * st + 1):
                g_put(k, 0, 0, hop, sign(k))
                g_put(k, 0, 0, hop, -sign(k))

    def g_take(st, level):
        for du, dv in LEVELS[level]:
            for k in (2 * st, 2 * st + 1):
                du_k, dv_k = du * sign(k), dv * sign(k)
                idx = gsem(k, du_k, dv_k)
                landed(g_chunk(k, du_k, dv_k), g_send.at[idx], g_recv.at[idx])
                if dv == 0:
                    if du == -1:
                        g_put(k, du_k, 0, 0, sign(k))
                    g_put(k, du_k, 0, 1, sign(k))
                    g_put(k, du_k, 0, 1, -sign(k))
                elif dv == -1:
                    g_put(k, du_k, dv_k, 1, sign(k))

    def pair_place(cls, dy):
        p = lax.rem(x + cls, 2)
        yy = md(y + dy, SIDE)
        q = yy * 2 + p
        lanes0 = (p * HALF_EXT + 2 * yy) * blk
        lanes1 = ((1 - p) * HALF_EXT + lax.rem(2 * yy + 4 + p, NB // 2)) * blk
        return q, al(lanes0, blk), (al(lanes0, blk), al(lanes1, blk))

    mt = pts // 3

    def density_pair(st, cls, dy):
        q, lane, span = pair_place(cls, dy)

        def step(i, carry):
            at = pl.ds(al(i * mt, mt), mt)
            prod = jnp.dot(
                rows_x[at, pl.ds(span[st], wide[st])], gath[st][q], preferred_element_type=F32
            )
            prod = prod * rows_x[at, pl.ds(lane, 2 * blk)].astype(F32)
            zacc[at, :] += prod[:, :blk] + prod[:, blk:]
            return carry

        lax.fori_loop(0, 3, step, 0)

    def both(level):
        for st in (0, 1):
            g_take(st, level)

    def density(cls, dy):
        density_pair(0, cls, dy)
        density_pair(1, cls, dy)

    pair_sums(0)
    g_start(0)
    pair_sums(1)
    g_start(1)
    both(0)
    density(1, 0)
    both(1)
    density(1, 1)
    g_take(0, 2)
    density(1, -1)
    g_take(1, 2)
    density(0, 0)
    density(0, 1)
    density(0, -1)
    density(1, 2)
    both(3)
    density(0, 2)

    total = count[0, 0]
    for i in range(pts // blk):
        at = pl.ds(i * blk, blk)
        dens_col = jnp.broadcast_to(jnp.sum(zacc[at, :], axis=1, keepdims=True), (blk, blk))
        inside = lax.broadcasted_iota(jnp.int32, (blk, blk), 0) + i * blk < total
        dens_col = jnp.where(inside, dens_col, 0.0)
        zacc[at, :] = dens_col
        scal[at, :] = jnp.where(
            inside, col3[2, at, :] * (col3[1, at, :] - col3[0, at, :] * dens_col), 0.0
        )

    def partial_pair(st, cls, dy):
        q, lane, span = pair_place(cls, dy)
        if st == 0:

            def scale(i, carry):
                at = pl.ds(al(i * blk, blk), blk)
                f = scal[at, :]
                v = rows_x[at, pl.ds(lane, 2 * blk)].astype(F32)
                scaled[q, at, :] = jnp.concatenate(
                    [v[:, :blk] * f, v[:, blk:] * f], axis=1
                ).astype(BF16)
                return carry

            lax.fori_loop(0, pts // blk, scale, 0, unroll=2)
        tile = wide[st] // 2

        def step(i, carry):
            o = pl.ds(al(span[st] + i * tile, 64), tile)
            v = jnp.dot(cols_x[o, :], scaled[q], preferred_element_type=F32)
            hpart[st][q, pl.ds(al(i * tile, 64), tile), :] = v.astype(BF16)
            return carry

        lax.fori_loop(0, 2, step, 0)

    def s_axes(k):
        return (1, 0) if k % 2 == 0 else (0, 1)

    def s_chunk(k, du, j):
        if k % 2 == 0:
            return chunk(hpart, j, md(y + du, SIDE), k)
        return chunk(hpart, md(x + du, SIDE), j, k)

    def buf(ref, k, *j):
        return ref.at[(k, *j, pl.ds(0, half[k // 2]))]

    def add_into(ref, *others):
        v = ref[...]
        for o in others:
            v = v + o[...]
        ref[...] = v

    def h_far(k, j):
        i = k * SIDE + j
        send(s_chunk(k, 2, j), buf(relay_in, k, j), s_send.at[i], s_recv.at[i],
             near(s_axes(k)[0], sign(k)))

    def h_direct(k, j):
        i = k * SIDE + j + 16
        send(s_chunk(k, -sign(k), j), buf(minus_in, k, j), s_send.at[i], s_recv.at[i],
             near(s_axes(k)[0], -sign(k)))

    def h_relay(k, j):
        i = k * SIDE + j
        ref = s_chunk(k, sign(k), j)
        landed(buf(relay_in, k, j), s_send.at[i], s_recv.at[i])
        add_into(ref, buf(relay_in, k, j))
        send(ref, buf(plus_in, k, j), s_send.at[32 + i], s_recv.at[32 + i],
             near(s_axes(k)[0], sign(k)))

    def v_at(k, dv):
        return md((x if k % 2 == 0 else y) + dv, SIDE)

    def h_sum(k, dv):
        j = v_at(k, dv)
        i = k * SIDE + j
        landed(buf(plus_in, k, j), s_send.at[32 + i], s_recv.at[32 + i])
        landed(buf(minus_in, k, j), s_send.at[16 + i], s_recv.at[16 + i])
        add_into(s_chunk(k, 0, j), buf(plus_in, k, j), buf(minus_in, k, j))

    def h2_far(k):
        send(s_chunk(k, 0, v_at(k, 2)), buf(relay2_in, k), s_send.at[48 + k], s_recv.at[48 + k],
             near(s_axes(k)[1], sign(k)))

    def h2_direct(k):
        send(s_chunk(k, 0, v_at(k, -sign(k))), buf(minus2_in, k), s_send.at[52 + k],
             s_recv.at[52 + k], near(s_axes(k)[1], -sign(k)))

    def h2_relay(k):
        ref = s_chunk(k, 0, v_at(k, sign(k)))
        landed(buf(relay2_in, k), s_send.at[48 + k], s_recv.at[48 + k])
        add_into(ref, buf(relay2_in, k))
        send(ref, buf(plus2_in, k), s_send.at[56 + k], s_recv.at[56 + k],
             near(s_axes(k)[1], sign(k)))

    def h2_sum(k):
        landed(buf(plus2_in, k), s_send.at[56 + k], s_recv.at[56 + k])
        landed(buf(minus2_in, k), s_send.at[52 + k], s_recv.at[52 + k])
        v = s_chunk(k, 0, v_at(k, 0))[...] + buf(plus2_in, k)[...] + buf(minus2_in, k)[...]
        st = k // 2
        final[pl.ds(st * stage_rows[0] + (k % 2) * half[st], half[st]), :] = v

    order = ((0, 2), (1, 2), (0, 1), (0, -1), (1, 1), (1, -1), (0, 0), (1, 0))

    late = []
    for cls, dy in order:
        partial_pair(0, cls, dy)
        partial_pair(1, cls, dy)
        due, late = late, []
        for dx in (2, 0) if cls == 0 else (1, -1):
            for k in quarters:
                du, j = (dy, v_at(k, dx)) if k % 2 == 0 else (dx, v_at(k, dy))
                if du == 2:
                    h_far(k, j)
                elif du == -sign(k):
                    h_direct(k, j)
                elif du == sign(k):
                    late.append((k, j))
        for k, j in due:
            h_relay(k, j)
    for k, j in late:
        h_relay(k, j)

    for k in quarters:
        h_sum(k, 2)
        h2_far(k)
    for k in quarters:
        h_sum(k, -sign(k))
        h2_direct(k)
    for k in quarters:
        h_sum(k, sign(k))
        h2_relay(k)
    for k in quarters:
        h_sum(k, 0)
    for i in range(pts // blk):
        at = pl.ds(i * blk, blk)
        n_out[0:1, at] = zacc[at, :].T[0:1, :]
    for k in quarters:
        h2_sum(k)

    def block(d):
        return final.at[pl.ds((d % 2) * stage_rows[0] + (d // 2) * blk, blk)]

    def mid_copy(d):
        return remote(
            block(d), mid.at[d - 1], m_send.at[d - 1], m_recv.at[d - 1], (m, partner(s, d))
        )

    def back_source(e):
        if e == 0:
            return block(0)
        if e < NB // 2:
            return flipped.at[e]
        return mid.at[NB - 1 - e]

    def back_copy(e):
        to = back_to(e)
        return remote(back_source(e), back.at[m], d_send.at[e], d_recv.at[m], (to, s))

    def back_to(e):
        if e < NB // 2:
            return partner(s, e)
        d = NB - e
        return md(s - d - NB // 2 * (d % 2), NB)

    def back_put(e):
        to = back_to(e)

        @pl.when(to != m)
        def _():
            back_copy(e).start()

        @pl.when(to == m)
        def _():
            back[m] = back_source(e)[...]

    for d in range(1, NOWN):
        mid_copy(d).start()
    for e in range(NB // 2):
        if e:
            flipped[e] = block(e)[...].astype(F32).T.astype(BF16)
        back_put(e)
    for d in range(1, NOWN):
        landed(mid.at[d - 1], m_send.at[d - 1], m_recv.at[d - 1])
        back_put(NB - d)

    for k in range(1, NB):
        first_copy(k).wait_send()

    @pl.when(jnp.logical_not(own))
    def _():
        first_copy(0).wait_send()

    for cp in sends:
        cp.wait_send()
    for d in range(1, NOWN):
        mid_copy(d).wait_send()

    for k in (15, 1, 14, 2, 13, 3, 12, 4, 11, 5, 10, 6, 9, 7, 8, 0):
        c = lax.rem(m + k, NB)
        if k:
            landed(back.at[c], d_send.at[0], d_recv.at[c])
        h_out[c] = back[c].astype(F32) * pattern[c, s, m].astype(F32)

    for e in range(NB):

        @pl.when(back_to(e) != m)
        def _():
            back_copy(e).wait_send()


def body(dens, basis, kern, pert, weight, count, active, pattern):
    blk = dens.shape[1]
    pts = basis.shape[1]
    nact = basis.shape[2] // blk
    wide0, wide1 = ((n + 1) * blk for n in STAGE_BLOCKS)
    half0 = STAGE_BLOCKS[0] * blk // 2
    vmem = pl.BlockSpec(memory_space=pltpu.VMEM)
    smem = pl.BlockSpec(memory_space=pltpu.SMEM)
    dma = pltpu.SemaphoreType.DMA
    return pl.pallas_call(
        _kernel,
        out_shape=(
            jax.ShapeDtypeStruct((NB, blk, blk), F32),
            jax.ShapeDtypeStruct((1, pts), F32),
        ),
        in_specs=[vmem, pl.BlockSpec(memory_space=pl.ANY), vmem, vmem, vmem, smem, smem, smem],
        out_specs=(vmem, vmem),
        scratch_shapes=[
            pltpu.VMEM((NB, blk, blk), BF16),
            pltpu.VMEM((nact, pts, blk), BF16),
            pltpu.VMEM((pts, 2 * HALF_EXT * blk), BF16),
            pltpu.VMEM((2 * HALF_EXT * blk, pts), BF16),
            pltpu.VMEM((NB // 2, wide0, 2 * blk), BF16),
            pltpu.VMEM((NB // 2, wide1, 2 * blk), BF16),
            pltpu.VMEM((pts, blk), F32),
            pltpu.VMEM((pts, blk), F32),
            pltpu.VMEM((3, pts, blk), F32),
            pltpu.VMEM((NB // 2, pts, 2 * blk), BF16),
            pltpu.VMEM((NB // 2, wide0, 2 * blk), BF16),
            pltpu.VMEM((NB // 2, wide1, 2 * blk), BF16),
            pltpu.VMEM((4, SIDE, half0, blk), BF16),
            pltpu.VMEM((4, SIDE, half0, blk), BF16),
            pltpu.VMEM((4, SIDE, half0, blk), BF16),
            pltpu.VMEM((4, half0, blk), BF16),
            pltpu.VMEM((4, half0, blk), BF16),
            pltpu.VMEM((4, half0, blk), BF16),
            pltpu.VMEM((NOWN * blk, blk), BF16),
            pltpu.VMEM((NB // 2, blk, blk), BF16),
            pltpu.VMEM((NB // 2, blk, blk), BF16),
            pltpu.VMEM((NB, blk, blk), BF16),
            dma((nact,)), dma((16,)), dma((16,)), dma((64,)), dma((64,)),
            dma((60,)), dma((60,)), dma((8,)), dma((8,)), dma((16,)), dma((16,)),
        ],
        compiler_params=pltpu.CompilerParams(
            collective_id=0, has_side_effects=True, vmem_limit_bytes=60 * 1024 * 1024
        ),
    )(
        dens, basis.reshape(basis.shape[1:]), kern, pert, weight, count,
        active.reshape(1, active.shape[-1]), pattern,
    )


def solution(mesh):
    placed = (
        P(None, "pts", "mat"),
        P("mat", "pts", None),
        P("mat", "pts"),
        P("mat", "pts"),
        P("mat", "pts"),
        P("mat", "pts"),
        P("mat", "pts", None),
        P(),
    )
    return jax.shard_map(
        body,
        mesh=mesh,
        in_specs=placed,
        out_specs=(P(None, "pts", "mat"), P("mat", "pts")),
        check_vma=False,
    )
```

```python
import jax
import jax.numpy as jnp
from jax import lax
from jax.experimental import pallas as pl
from jax.experimental.pallas import tpu as pltpu
from jax.sharding import PartitionSpec as P

NB = 16
SIDE = 4
NOWN = 9
MESH = pl.DeviceIdType.MESH
F32 = jnp.float32
BF16 = jnp.bfloat16


STAGE_BLOCKS = (5, 4)
HALF_EXT = 12
LEVELS = (
    ((-1, 0), (0, -1), (1, 0), (0, 1)),
    ((2, 0), (-1, -1), (1, -1), (-1, 1), (1, 1)),
    ((2, -1), (0, 2), (2, 1), (-1, 2), (1, 2)),
    ((2, 2),),
)


def _kernel(
    dens_in, basis, kern_in, pert_in, weight_in, count, active, pattern_in,
    h_out, n_out,
    dens, line3, pattern, first, packed, rows_x, cols_x, gath0, gath1, zacc, scal, col3, scaled, hpart0, hpart1,
    relay_in, plus_in, minus_in, relay2_in, plus2_in, minus2_in,
    final, flipped, mid, back, masked, n_line,
    basis_sem, in_sem, a_send, a_recv, g_send, g_recv, s_send, s_recv,
    m_send, m_recv, d_send, d_recv, out_sem,
):
    blk = dens_in.shape[1]
    nact, pts = packed.shape[0], packed.shape[1]
    gath = (gath0, gath1)
    hpart = (hpart0, hpart1)
    stage_rows = [n * blk for n in STAGE_BLOCKS]
    half = [n // 2 for n in stage_rows]
    wide = [n + blk for n in stage_rows]
    m = lax.axis_index("mat")
    s = lax.axis_index("pts")
    x = lax.rem(s, SIDE)
    y = lax.div(s, SIDE)

    def md(v, n):
        return lax.rem(v + 2 * n, n)

    def partner(t, d):
        return lax.rem(t + d + NB // 2 * (d % 2), NB)

    def al(v, k):
        return pl.multiple_of(v, k)

    def near(axis, step):
        if axis == 0:
            return (m, y * SIDE + md(x + step, SIDE))
        return (m, md(y + step, SIDE) * SIDE + x)

    quarters = range(4)

    def sign(k):
        return 1 if k < 2 else -1

    def chunk(bufs, xx, yy, k):
        h = half[k // 2]
        return bufs[k // 2].at[yy * SIDE + xx, pl.ds((k % 2) * h, h)]

    def remote(src, dst, ssem, rsem, dev):
        return pltpu.make_async_remote_copy(
            src_ref=src, dst_ref=dst, send_sem=ssem, recv_sem=rsem,
            device_id=dev, device_id_type=MESH,
        )

    sends = []

    def send(src, dst, ssem, rsem, dev):
        cp = remote(src, dst, ssem, rsem, dev)
        cp.start()
        sends.append(cp)

    def landed(dst, ssem, rsem):
        remote(dst, dst, ssem, rsem, (m, s)).wait_recv()

    loads = [
        pltpu.make_async_copy(basis.at[:, pl.ds(j * blk, blk)], packed.at[j], basis_sem.at[j])
        for j in range(nact)
    ]
    dens_load = pltpu.make_async_copy(dens_in, dens, in_sem.at[0])
    dens_load.start()
    small = [
        pltpu.make_async_copy(ref, line3.at[j], in_sem.at[1 + j])
        for j, ref in enumerate((kern_in, pert_in, weight_in))
    ]
    small.append(pltpu.make_async_copy(pattern_in, pattern, in_sem.at[4]))
    for cp in small + loads:
        cp.start()
    diff = md(m - s, NB)
    diff = lax.rem(diff + NB // 2 * lax.rem(diff, 2), NB)
    own = diff < NB // 2
    other = jnp.where(own, s, m)

    barrier = pltpu.get_barrier_semaphore()
    for d in range(NB // 2):
        src = partner(s, d)

        @pl.when(src != m)
        def _():
            pl.semaphore_signal(barrier, inc=1, device_id=(src, s), device_id_type=MESH)

    for d in range(1, NOWN):
        pl.semaphore_signal(
            barrier, inc=1, device_id=(s, partner(s, d)), device_id_type=MESH
        )
    for axis in (0, 1):
        for step in (1, -1):
            pl.semaphore_signal(barrier, inc=1, device_id=near(axis, step), device_id_type=MESH)
    dens_load.wait()
    pl.semaphore_wait(barrier, NB + 4 - own.astype(jnp.int32))

    slot = jnp.where(own, diff, NB + NB // 2 - 1 - diff)

    def first_copy(k):
        c = lax.rem(m + k, NB)
        return remote(dens.at[c], first.at[slot], a_send.at[k], a_recv.at[slot], (c, other))

    def first_sends():
        for k in (8, 7, 9, 6, 10, 5, 11, 4, 12, 3, 13, 2, 14, 1, 15):
            first_copy(k).start()

        @pl.when(jnp.logical_not(own))
        def _():
            first_copy(0).start()

        @pl.when(own)
        def _():
            first[diff] = dens[m]

    first_sends()

    zacc[...] = jnp.zeros_like(zacc)
    for cp in small:
        cp.wait()
    for i in range(pts // blk):
        at = pl.ds(i * blk, blk)
        for j in range(3):
            col3[j, at, :] = jnp.broadcast_to(line3[j, 0:1, at], (blk, blk)).T
    for cp in loads:
        cp.wait()
    part = pts // 3

    def spread(a, carry):
        pos = jnp.int32(0)
        hits = jnp.int32(0)
        for j in range(nact):
            hit = (active[0, j] == a).astype(jnp.int32)
            pos = pos + j * hit
            hits = hits + hit
        pos = jnp.minimum(pos, nact - 1)
        lead = lax.div(a, 2)
        to = lax.rem(a, 2) * HALF_EXT + lead
        for i in range(3):
            at = pl.ds(i * part, part)
            v = packed[pos, at, :]
            v = jnp.where(hits > 0, v, jnp.zeros_like(v))
            vt = v.T
            rows_x[at, pl.ds(al(to * blk, blk), blk)] = v
            cols_x[pl.ds(al(to * blk, blk), blk), at] = vt

            @pl.when(lead < HALF_EXT - NB // 2)
            def _():
                again = to + NB // 2
                rows_x[at, pl.ds(al(again * blk, blk), blk)] = v
                cols_x[pl.ds(al(again * blk, blk), blk), at] = vt

        return carry

    lax.fori_loop(0, NB, spread, 0)

    def first_landed(j):
        landed(first.at[j], a_send.at[0], a_recv.at[j])

    def pat(a, b):
        return pattern[m, a, b].astype(F32)

    def pair_sums(st):
        for d in range(st, NOWN, 2):
            sd = partner(s, d)
            if d < NB // 2:

                @pl.when(sd != m)
                def _():
                    first_landed(d)

            if d >= 1:
                first_landed(NB // 2 - 1 + d)
            if d == 0:
                v = first[0].astype(F32) * pat(s, s)
            else:
                v = first[NB // 2 - 1 + d].astype(F32) * pat(sd, s)
                if d < NB // 2:
                    v = v + (first[d].astype(F32) * pat(s, sd)).T
            gath[st][s, pl.ds(d // 2 * blk, blk), :] = v.astype(BF16)

    def g_axes(k):
        return (0, 1) if k % 2 == 0 else (1, 0)

    def g_chunk(k, du, dv):
        dx, dy = (du, dv) if k % 2 == 0 else (dv, du)
        return chunk(gath, md(x + dx, SIDE), md(y + dy, SIDE), k)

    def gsem(k, du, dv):
        return k * 16 + (du % SIDE) * SIDE + dv % SIDE

    def g_put(k, du, dv, hop, step):
        ref = g_chunk(k, du, dv)
        idx = gsem(k, du - step, dv) if hop == 0 else gsem(k, du, dv - step)
        send(ref, ref, g_send.at[idx], g_recv.at[idx], near(g_axes(k)[hop], step))

    def g_start(st):
        for hop in (0, 1):
            for k in (2 * st, 2 * st + 1):
                g_put(k, 0, 0, hop, sign(k))
                g_put(k, 0, 0, hop, -sign(k))

    def g_take(st, level):
        for du, dv in LEVELS[level]:
            for k in (2 * st, 2 * st + 1):
                du_k, dv_k = du * sign(k), dv * sign(k)
                idx = gsem(k, du_k, dv_k)
                landed(g_chunk(k, du_k, dv_k), g_send.at[idx], g_recv.at[idx])
                if dv == 0:
                    if du == -1:
                        g_put(k, du_k, 0, 0, sign(k))
                    g_put(k, du_k, 0, 1, sign(k))
                    g_put(k, du_k, 0, 1, -sign(k))
                elif dv == -1:
                    g_put(k, du_k, dv_k, 1, sign(k))

    def pair_place(cls, dy):
        p = lax.rem(x + cls, 2)
        yy = md(y + dy, SIDE)
        q = yy * SIDE + p
        lanes0 = (p * HALF_EXT + 2 * yy) * blk
        lanes1 = ((1 - p) * HALF_EXT + lax.rem(2 * yy + 4 + p, NB // 2)) * blk
        return q, al(lanes0, blk), (al(lanes0, blk), al(lanes1, blk))

    def side_by_side(ref, q):
        zero = jnp.zeros((blk, blk), BF16)
        return jnp.concatenate(
            [
                jnp.concatenate([ref[q], zero], axis=0),
                jnp.concatenate([zero, ref[q + 2]], axis=0),
            ],
            axis=1,
        )

    def density_pair(st, cls, dy):
        q, lane, span = pair_place(cls, dy)

        prod = jnp.dot(
            rows_x[:, pl.ds(span[st], wide[st])], side_by_side(gath[st], q), preferred_element_type=F32
        )
        prod = prod * rows_x[:, pl.ds(lane, 2 * blk)].astype(F32)
        zacc[...] += prod[:, :blk] + prod[:, blk:]

    def both(level):
        for st in (0, 1):
            g_take(st, level)

    def density(cls, dy):
        density_pair(0, cls, dy)
        density_pair(1, cls, dy)

    pair_sums(0)
    g_start(0)
    pair_sums(1)
    g_start(1)
    both(0)
    density(1, 0)
    both(1)
    density(1, 1)
    g_take(0, 2)
    density(1, -1)
    g_take(1, 2)
    density(0, 0)
    density(0, 1)
    density(0, -1)
    density(1, 2)
    both(3)
    density(0, 2)

    total = count[0, 0]
    for i in range(pts // blk):
        at = pl.ds(i * blk, blk)
        dens_col = jnp.broadcast_to(jnp.sum(zacc[at, :], axis=1, keepdims=True), (blk, blk))
        inside = lax.broadcasted_iota(jnp.int32, (blk, blk), 0) + i * blk < total
        dens_col = jnp.where(inside, dens_col, 0.0)
        zacc[at, :] = dens_col
        scal[at, :] = jnp.where(
            inside, col3[2, at, :] * (col3[1, at, :] - col3[0, at, :] * dens_col), 0.0
        )

    def partial_pair(st, cls, dy):
        q, lane, span = pair_place(cls, dy)
        if st == 0:

            def scale(i, carry):
                at = pl.ds(al(i * blk, blk), blk)
                f = scal[at, :]
                v = rows_x[at, pl.ds(lane, 2 * blk)].astype(F32)
                scaled[at, :] = jnp.concatenate(
                    [v[:, :blk] * f, v[:, blk:] * f], axis=1
                ).astype(BF16)
                return carry

            lax.fori_loop(0, pts // blk, scale, 0, unroll=2)
        v = jnp.dot(cols_x[pl.ds(span[st], wide[st]), :], scaled[...], preferred_element_type=F32)
        hpart[st][q] = v[: stage_rows[st], :blk].astype(BF16)
        hpart[st][q + 2] = v[blk:, blk:].astype(BF16)

    def s_axes(k):
        return (1, 0) if k % 2 == 0 else (0, 1)

    def s_chunk(k, du, j):
        if k % 2 == 0:
            return chunk(hpart, j, md(y + du, SIDE), k)
        return chunk(hpart, md(x + du, SIDE), j, k)

    def buf(ref, k, *j):
        return ref.at[(k, *j, pl.ds(0, half[k // 2]))]

    def add_into(ref, *others):
        v = ref[...]
        for o in others:
            v = v + o[...]
        ref[...] = v

    def h_far(k, j):
        i = k * SIDE + j
        send(s_chunk(k, 2, j), buf(relay_in, k, j), s_send.at[i], s_recv.at[i],
             near(s_axes(k)[0], sign(k)))

    def h_direct(k, j):
        i = k * SIDE + j + 16
        send(s_chunk(k, -sign(k), j), buf(minus_in, k, j), s_send.at[i], s_recv.at[i],
             near(s_axes(k)[0], -sign(k)))

    def h_relay(k, j):
        i = k * SIDE + j
        ref = s_chunk(k, sign(k), j)
        landed(buf(relay_in, k, j), s_send.at[i], s_recv.at[i])
        add_into(ref, buf(relay_in, k, j))
        send(ref, buf(plus_in, k, j), s_send.at[32 + i], s_recv.at[32 + i],
             near(s_axes(k)[0], sign(k)))

    def v_at(k, dv):
        return md((x if k % 2 == 0 else y) + dv, SIDE)

    def h_sum(k, dv):
        j = v_at(k, dv)
        i = k * SIDE + j
        landed(buf(plus_in, k, j), s_send.at[32 + i], s_recv.at[32 + i])
        landed(buf(minus_in, k, j), s_send.at[16 + i], s_recv.at[16 + i])
        add_into(s_chunk(k, 0, j), buf(plus_in, k, j), buf(minus_in, k, j))

    def h2_far(k):
        send(s_chunk(k, 0, v_at(k, 2)), buf(relay2_in, k), s_send.at[48 + k], s_recv.at[48 + k],
             near(s_axes(k)[1], sign(k)))

    def h2_direct(k):
        send(s_chunk(k, 0, v_at(k, -sign(k))), buf(minus2_in, k), s_send.at[52 + k],
             s_recv.at[52 + k], near(s_axes(k)[1], -sign(k)))

    def h2_relay(k):
        ref = s_chunk(k, 0, v_at(k, sign(k)))
        landed(buf(relay2_in, k), s_send.at[48 + k], s_recv.at[48 + k])
        add_into(ref, buf(relay2_in, k))
        send(ref, buf(plus2_in, k), s_send.at[56 + k], s_recv.at[56 + k],
             near(s_axes(k)[1], sign(k)))

    def h2_sum(k):
        landed(buf(plus2_in, k), s_send.at[56 + k], s_recv.at[56 + k])
        landed(buf(minus2_in, k), s_send.at[52 + k], s_recv.at[52 + k])
        v = s_chunk(k, 0, v_at(k, 0))[...] + buf(plus2_in, k)[...] + buf(minus2_in, k)[...]
        st = k // 2
        final[pl.ds(st * stage_rows[0] + (k % 2) * half[st], half[st]), :] = v

    order = ((0, 2), (1, 2), (0, 1), (0, -1), (1, 1), (1, -1), (0, 0), (1, 0))

    late = []
    for cls, dy in order:
        partial_pair(0, cls, dy)
        partial_pair(1, cls, dy)
        due, late = late, []
        for dx in (2, 0) if cls == 0 else (1, -1):
            for k in quarters:
                du, j = (dy, v_at(k, dx)) if k % 2 == 0 else (dx, v_at(k, dy))
                if du == 2:
                    h_far(k, j)
                elif du == -sign(k):
                    h_direct(k, j)
                elif du == sign(k):
                    late.append((k, j))
        for k, j in due:
            h_relay(k, j)
    for k, j in late:
        h_relay(k, j)

    for k in quarters:
        h_sum(k, 2)
        h2_far(k)
    for k in quarters:
        h_sum(k, -sign(k))
        h2_direct(k)
    for k in quarters:
        h_sum(k, sign(k))
        h2_relay(k)
    for k in quarters:
        h_sum(k, 0)
    for i in range(pts // blk):
        at = pl.ds(i * blk, blk)
        n_line[0:1, at] = zacc[at, :].T[0:1, :]
    n_copy = pltpu.make_async_copy(n_line, n_out, in_sem.at[5])
    n_copy.start()
    for k in quarters:
        h2_sum(k)

    def block(d):
        return final.at[pl.ds((d % 2) * stage_rows[0] + (d // 2) * blk, blk)]

    def mid_copy(d):
        return remote(
            block(d), mid.at[d - 1], m_send.at[d - 1], m_recv.at[d - 1], (m, partner(s, d))
        )

    def back_source(e):
        if e == 0:
            return block(0)
        if e < NB // 2:
            return flipped.at[e]
        return mid.at[NB - 1 - e]

    def back_copy(e):
        to = back_to(e)
        return remote(back_source(e), back.at[m], d_send.at[e], d_recv.at[m], (to, s))

    def back_to(e):
        if e < NB // 2:
            return partner(s, e)
        d = NB - e
        return md(s - d - NB // 2 * (d % 2), NB)

    def back_put(e):
        to = back_to(e)

        @pl.when(to != m)
        def _():
            back_copy(e).start()

        @pl.when(to == m)
        def _():
            back[m] = back_source(e)[...]

    for d in range(1, NOWN):
        mid_copy(d).start()
    for e in range(NB // 2):
        if e:
            flipped[e] = block(e)[...].astype(F32).T.astype(BF16)
        back_put(e)
    for d in range(1, NOWN):
        landed(mid.at[d - 1], m_send.at[d - 1], m_recv.at[d - 1])
        back_put(NB - d)

    def h_copy(c):
        return pltpu.make_async_copy(masked.at[c], h_out.at[c], out_sem.at[c])

    for k in range(1, NB):
        first_copy(k).wait_send()

    @pl.when(jnp.logical_not(own))
    def _():
        first_copy(0).wait_send()

    for cp in sends:
        cp.wait_send()
    for d in range(1, NOWN):
        mid_copy(d).wait_send()

    for k in (15, 1, 14, 2, 13, 3, 12, 4, 11, 5, 10, 6, 9, 7, 8, 0):
        c = lax.rem(m + k, NB)
        if k:
            landed(back.at[c], d_send.at[0], d_recv.at[c])
        masked[c] = (back[c].astype(F32) * pattern[c, s, m].astype(F32)).astype(BF16)
        h_copy(c).start()

    for e in range(NB):

        @pl.when(back_to(e) != m)
        def _():
            back_copy(e).wait_send()

    n_copy.wait()
    for c in range(NB):
        h_copy(c).wait()


def _widen(h_low, n_row, h_out, n_out):
    h_out[...] = h_low[...].astype(F32)
    n_out[...] = n_row[...]


def body(dens, basis, kern, pert, weight, count, active, pattern):
    blk = dens.shape[1]
    pts = basis.shape[1]
    nact = basis.shape[2] // blk
    rows0, rows1 = (n * blk for n in STAGE_BLOCKS)
    half0 = STAGE_BLOCKS[0] * blk // 2
    vmem = pl.BlockSpec(memory_space=pltpu.VMEM)
    smem = pl.BlockSpec(memory_space=pltpu.SMEM)
    dma = pltpu.SemaphoreType.DMA
    anywhere = pl.BlockSpec(memory_space=pl.ANY)
    h_low, n_row = pl.pallas_call(
        _kernel,
        out_shape=(
            jax.ShapeDtypeStruct((NB, blk, blk), BF16),
            jax.ShapeDtypeStruct((1, pts), F32),
        ),
        in_specs=[anywhere] * 5 + [smem, smem, anywhere],
        out_specs=(anywhere, anywhere),
        scratch_shapes=[
            pltpu.VMEM((NB, blk, blk), BF16),
            pltpu.VMEM((3, 1, pts), F32),
            pltpu.SMEM(pattern.shape, jnp.int32),
            pltpu.VMEM((NB, blk, blk), BF16),
            pltpu.VMEM((nact, pts, blk), BF16),
            pltpu.VMEM((pts, 2 * HALF_EXT * blk), BF16),
            pltpu.VMEM((2 * HALF_EXT * blk, pts), BF16),
            pltpu.VMEM((NB, rows0, blk), BF16),
            pltpu.VMEM((NB, rows1, blk), BF16),
            pltpu.VMEM((pts, blk), F32),
            pltpu.VMEM((pts, blk), F32),
            pltpu.VMEM((3, pts, blk), F32),
            pltpu.VMEM((pts, 2 * blk), BF16),
            pltpu.VMEM((NB, rows0, blk), BF16),
            pltpu.VMEM((NB, rows1, blk), BF16),
            pltpu.VMEM((4, SIDE, half0, blk), BF16),
            pltpu.VMEM((4, SIDE, half0, blk), BF16),
            pltpu.VMEM((4, SIDE, half0, blk), BF16),
            pltpu.VMEM((4, half0, blk), BF16),
            pltpu.VMEM((4, half0, blk), BF16),
            pltpu.VMEM((4, half0, blk), BF16),
            pltpu.VMEM((NOWN * blk, blk), BF16),
            pltpu.VMEM((NB // 2, blk, blk), BF16),
            pltpu.VMEM((NB // 2, blk, blk), BF16),
            pltpu.VMEM((NB, blk, blk), BF16),
            pltpu.VMEM((NB, blk, blk), BF16),
            pltpu.VMEM((1, pts), F32),
            dma((nact,)), dma((6,)), dma((16,)), dma((16,)), dma((64,)), dma((64,)),
            dma((60,)), dma((60,)), dma((8,)), dma((8,)), dma((16,)), dma((16,)), dma((16,)),
        ],
        compiler_params=pltpu.CompilerParams(
            collective_id=0, has_side_effects=True, vmem_limit_bytes=60 * 1024 * 1024
        ),
    )(
        dens, basis.reshape(basis.shape[1:]), kern, pert, weight, count,
        active.reshape(1, active.shape[-1]), pattern,
    )
    return pl.pallas_call(
        _widen,
        out_shape=(
            jax.ShapeDtypeStruct(h_low.shape, F32),
            jax.ShapeDtypeStruct(n_row.shape, F32),
        ),
        in_specs=[vmem, vmem],
        out_specs=(vmem, vmem),
    )(h_low, n_row)


def solution(mesh):
    placed = (
        P(None, "pts", "mat"),
        P("mat", "pts", None),
        P("mat", "pts"),
        P("mat", "pts"),
        P("mat", "pts"),
        P("mat", "pts"),
        P("mat", "pts", None),
        P(),
    )
    return jax.shard_map(
        body,
        mesh=mesh,
        in_specs=placed,
        out_specs=(P(None, "pts", "mat"), P("mat", "pts")),
        check_vma=False,
    )
```

```python
import jax
import jax.numpy as jnp
from jax import lax
from jax.experimental import pallas as pl
from jax.experimental.pallas import tpu as pltpu
from jax.sharding import PartitionSpec as P

NB = 16
SIDE = 4
NOWN = 9
MESH = pl.DeviceIdType.MESH
F32 = jnp.float32
BF16 = jnp.bfloat16


STAGE_BLOCKS = (5, 4)
HALF_EXT = 12
LEVELS = (
    ((-1, 0), (0, -1), (1, 0), (0, 1)),
    ((2, 0), (-1, -1), (1, -1), (-1, 1), (1, 1)),
    ((2, -1), (0, 2)),
    ((2, 1), (-1, 2), (1, 2)),
    ((2, 2),),
)


def _kernel(
    dens_in, basis, kern_in, pert_in, weight_in, count, active, pattern_in,
    h_out, n_out,
    dens, line3, pattern, first, packed, rows_x, cols_x, gath0, gath1, zacc, scal, col3, scaled, hpart0, hpart1,
    relay_in, plus_in, minus_in, relay2_in, plus2_in, minus2_in,
    final, flipped, mid, back, masked, n_line,
    basis_sem, in_sem, a_send, a_recv, g_send, g_recv, s_send, s_recv,
    m_send, m_recv, d_send, d_recv, out_sem,
):
    blk = dens_in.shape[1]
    nact, pts = packed.shape[0], packed.shape[1]
    gath = (gath0, gath1)
    hpart = (hpart0, hpart1)
    stage_rows = [n * blk for n in STAGE_BLOCKS]
    half = [n // 2 for n in stage_rows]
    wide = [n + blk for n in stage_rows]
    m = lax.axis_index("mat")
    s = lax.axis_index("pts")
    x = lax.rem(s, SIDE)
    y = lax.div(s, SIDE)

    def md(v, n):
        return lax.rem(v + 2 * n, n)

    def partner(t, d):
        return lax.rem(t + d + NB // 2 * (d % 2), NB)

    def al(v, k):
        return pl.multiple_of(v, k)

    def near(axis, step):
        if axis == 0:
            return (m, y * SIDE + md(x + step, SIDE))
        return (m, md(y + step, SIDE) * SIDE + x)

    quarters = range(4)

    def sign(k):
        return 1 if k < 2 else -1

    def chunk(bufs, xx, yy, k):
        h = half[k // 2]
        return bufs[k // 2].at[yy * SIDE + xx, pl.ds((k % 2) * h, h)]

    def remote(src, dst, ssem, rsem, dev):
        return pltpu.make_async_remote_copy(
            src_ref=src, dst_ref=dst, send_sem=ssem, recv_sem=rsem,
            device_id=dev, device_id_type=MESH,
        )

    sends = []

    def send(src, dst, ssem, rsem, dev):
        cp = remote(src, dst, ssem, rsem, dev)
        cp.start()
        sends.append(cp)

    def landed(dst, ssem, rsem):
        remote(dst, dst, ssem, rsem, (m, s)).wait_recv()

    loads = [
        pltpu.make_async_copy(basis.at[:, pl.ds(j * blk, blk)], packed.at[j], basis_sem.at[j])
        for j in range(nact)
    ]
    dens_load = pltpu.make_async_copy(dens_in, dens, in_sem.at[0])
    dens_load.start()
    small = [
        pltpu.make_async_copy(ref, line3.at[j], in_sem.at[1 + j])
        for j, ref in enumerate((kern_in, pert_in, weight_in))
    ]
    small.append(pltpu.make_async_copy(pattern_in, pattern, in_sem.at[4]))
    for cp in small + loads:
        cp.start()
    diff = md(m - s, NB)
    diff = lax.rem(diff + NB // 2 * lax.rem(diff, 2), NB)
    own = diff < NB // 2
    other = jnp.where(own, s, m)

    barrier = pltpu.get_barrier_semaphore()
    for d in range(NB // 2):
        src = partner(s, d)

        @pl.when(src != m)
        def _():
            pl.semaphore_signal(barrier, inc=1, device_id=(src, s), device_id_type=MESH)

    for d in range(1, NOWN):
        pl.semaphore_signal(
            barrier, inc=1, device_id=(s, partner(s, d)), device_id_type=MESH
        )
    for axis in (0, 1):
        for step in (1, -1):
            pl.semaphore_signal(barrier, inc=1, device_id=near(axis, step), device_id_type=MESH)
    dens_load.wait()
    pl.semaphore_wait(barrier, NB + 4 - own.astype(jnp.int32))

    slot = jnp.where(own, diff, NB + NB // 2 - 1 - diff)

    def first_copy(k):
        c = lax.rem(m + k, NB)
        return remote(dens.at[c], first.at[slot], a_send.at[k], a_recv.at[slot], (c, other))

    def first_sends():
        for k in (8, 7, 9, 6, 10, 5, 11, 4, 12, 3, 13, 2, 14, 1, 15):
            first_copy(k).start()

        @pl.when(jnp.logical_not(own))
        def _():
            first_copy(0).start()

        @pl.when(own)
        def _():
            first[diff] = dens[m]

    first_sends()

    zacc[...] = jnp.zeros_like(zacc)
    for cp in small:
        cp.wait()
    for i in range(pts // blk):
        at = pl.ds(i * blk, blk)
        for j in range(3):
            col3[j, at, :] = jnp.broadcast_to(line3[j, 0:1, at], (blk, blk)).T
    for cp in loads:
        cp.wait()
    part = pts // 3

    def spread(a, carry):
        pos = jnp.int32(0)
        hits = jnp.int32(0)
        for j in range(nact):
            hit = (active[0, j] == a).astype(jnp.int32)
            pos = pos + j * hit
            hits = hits + hit
        pos = jnp.minimum(pos, nact - 1)
        lead = lax.div(a, 2)
        to = lax.rem(a, 2) * HALF_EXT + lead
        for i in range(3):
            at = pl.ds(i * part, part)
            v = packed[pos, at, :]
            v = jnp.where(hits > 0, v, jnp.zeros_like(v))
            vt = v.T
            rows_x[at, pl.ds(al(to * blk, blk), blk)] = v
            cols_x[pl.ds(al(to * blk, blk), blk), at] = vt

            @pl.when(lead < HALF_EXT - NB // 2)
            def _():
                again = to + NB // 2
                rows_x[at, pl.ds(al(again * blk, blk), blk)] = v
                cols_x[pl.ds(al(again * blk, blk), blk), at] = vt

        return carry

    lax.fori_loop(0, NB, spread, 0)

    def first_landed(j):
        landed(first.at[j], a_send.at[0], a_recv.at[j])

    def pat(a, b):
        return pattern[m, a, b].astype(F32)

    def pair_sums(st):
        for d in range(st, NOWN, 2):
            sd = partner(s, d)
            if d < NB // 2:

                @pl.when(sd != m)
                def _():
                    first_landed(d)

            if d >= 1:
                first_landed(NB // 2 - 1 + d)
            if d == 0:
                v = first[0].astype(F32) * pat(s, s)
            else:
                v = first[NB // 2 - 1 + d].astype(F32) * pat(sd, s)
                if d < NB // 2:
                    v = v + (first[d].astype(F32) * pat(s, sd)).T
            gath[st][s, pl.ds(d // 2 * blk, blk), :] = v.astype(BF16)

    def g_axes(k):
        return (0, 1) if k % 2 == 0 else (1, 0)

    def g_chunk(k, du, dv):
        dx, dy = (du, dv) if k % 2 == 0 else (dv, du)
        return chunk(gath, md(x + dx, SIDE), md(y + dy, SIDE), k)

    def gsem(k, du, dv):
        return k * 16 + (du % SIDE) * SIDE + dv % SIDE

    def g_put(k, du, dv, hop, step):
        ref = g_chunk(k, du, dv)
        idx = gsem(k, du - step, dv) if hop == 0 else gsem(k, du, dv - step)
        send(ref, ref, g_send.at[idx], g_recv.at[idx], near(g_axes(k)[hop], step))

    def g_start(st):
        for hop in (0, 1):
            for k in (2 * st, 2 * st + 1):
                g_put(k, 0, 0, hop, sign(k))
                g_put(k, 0, 0, hop, -sign(k))

    def g_take(st, level):
        for du, dv in LEVELS[level]:
            for k in (2 * st, 2 * st + 1):
                du_k, dv_k = du * sign(k), dv * sign(k)
                idx = gsem(k, du_k, dv_k)
                landed(g_chunk(k, du_k, dv_k), g_send.at[idx], g_recv.at[idx])
                if dv == 0:
                    if du == -1:
                        g_put(k, du_k, 0, 0, sign(k))
                    g_put(k, du_k, 0, 1, sign(k))
                    g_put(k, du_k, 0, 1, -sign(k))
                elif dv == -1:
                    g_put(k, du_k, dv_k, 1, sign(k))

    def pair_place(cls, dy):
        p = lax.rem(x + cls, 2)
        yy = md(y + dy, SIDE)
        q = yy * SIDE + p
        lanes0 = (p * HALF_EXT + 2 * yy) * blk
        lanes1 = ((1 - p) * HALF_EXT + lax.rem(2 * yy + 4 + p, NB // 2)) * blk
        return q, al(lanes0, blk), (al(lanes0, blk), al(lanes1, blk))

    def side_by_side(ref, q):
        zero = jnp.zeros((blk, blk), BF16)
        return jnp.concatenate(
            [
                jnp.concatenate([ref[q], zero], axis=0),
                jnp.concatenate([zero, ref[q + 2]], axis=0),
            ],
            axis=1,
        )

    def density_pair(st, cls, dy):
        q, lane, span = pair_place(cls, dy)

        prod = jnp.dot(
            rows_x[:, pl.ds(span[st], wide[st])], side_by_side(gath[st], q), preferred_element_type=F32
        )
        prod = prod * rows_x[:, pl.ds(lane, 2 * blk)].astype(F32)
        zacc[...] += prod[:, :blk] + prod[:, blk:]

    def both(level):
        for st in (0, 1):
            g_take(st, level)

    def density(cls, dy):
        density_pair(0, cls, dy)
        density_pair(1, cls, dy)

    pair_sums(0)
    g_start(0)
    pair_sums(1)
    g_start(1)
    both(0)
    density(1, 0)
    both(1)
    density(1, 1)
    both(2)
    density(1, -1)
    density(0, 0)
    g_take(0, 3)
    density_pair(0, 0, 1)
    density_pair(0, 0, -1)
    g_take(1, 3)
    density_pair(0, 1, 2)
    density_pair(1, 0, 1)
    density_pair(1, 0, -1)
    density_pair(1, 1, 2)
    g_take(0, 4)
    density_pair(0, 0, 2)
    g_take(1, 4)
    density_pair(1, 0, 2)

    total = count[0, 0]
    for i in range(pts // blk):
        at = pl.ds(i * blk, blk)
        dens_col = jnp.broadcast_to(jnp.sum(zacc[at, :], axis=1, keepdims=True), (blk, blk))
        inside = lax.broadcasted_iota(jnp.int32, (blk, blk), 0) + i * blk < total
        dens_col = jnp.where(inside, dens_col, 0.0)
        zacc[at, :] = dens_col
        scal[at, :] = jnp.where(
            inside, col3[2, at, :] * (col3[1, at, :] - col3[0, at, :] * dens_col), 0.0
        )

    def partial_pair(st, cls, dy):
        q, lane, span = pair_place(cls, dy)
        if st == 0:

            def scale(i, carry):
                at = pl.ds(al(i * blk, blk), blk)
                f = scal[at, :]
                v = rows_x[at, pl.ds(lane, 2 * blk)].astype(F32)
                scaled[at, :] = jnp.concatenate(
                    [v[:, :blk] * f, v[:, blk:] * f], axis=1
                ).astype(BF16)
                return carry

            lax.fori_loop(0, pts // blk, scale, 0, unroll=2)
        v = jnp.dot(cols_x[pl.ds(span[st], wide[st]), :], scaled[...], preferred_element_type=F32)
        hpart[st][q] = v[: stage_rows[st], :blk].astype(BF16)
        hpart[st][q + 2] = v[blk:, blk:].astype(BF16)

    def s_axes(k):
        return (1, 0) if k % 2 == 0 else (0, 1)

    def s_chunk(k, du, j):
        if k % 2 == 0:
            return chunk(hpart, j, md(y + du, SIDE), k)
        return chunk(hpart, md(x + du, SIDE), j, k)

    def buf(ref, k, *j):
        return ref.at[(k, *j, pl.ds(0, half[k // 2]))]

    def add_into(ref, *others):
        v = ref[...]
        for o in others:
            v = v + o[...]
        ref[...] = v

    def h_far(k, j):
        i = k * SIDE + j
        send(s_chunk(k, 2, j), buf(relay_in, k, j), s_send.at[i], s_recv.at[i],
             near(s_axes(k)[0], sign(k)))

    def h_direct(k, j):
        i = k * SIDE + j + 16
        send(s_chunk(k, -sign(k), j), buf(minus_in, k, j), s_send.at[i], s_recv.at[i],
             near(s_axes(k)[0], -sign(k)))

    def h_relay(k, j):
        i = k * SIDE + j
        ref = s_chunk(k, sign(k), j)
        landed(buf(relay_in, k, j), s_send.at[i], s_recv.at[i])
        add_into(ref, buf(relay_in, k, j))
        send(ref, buf(plus_in, k, j), s_send.at[32 + i], s_recv.at[32 + i],
             near(s_axes(k)[0], sign(k)))

    def v_at(k, dv):
        return md((x if k % 2 == 0 else y) + dv, SIDE)

    def h_sum(k, dv):
        j = v_at(k, dv)
        i = k * SIDE + j
        landed(buf(plus_in, k, j), s_send.at[32 + i], s_recv.at[32 + i])
        landed(buf(minus_in, k, j), s_send.at[16 + i], s_recv.at[16 + i])
        add_into(s_chunk(k, 0, j), buf(plus_in, k, j), buf(minus_in, k, j))

    def h2_far(k):
        send(s_chunk(k, 0, v_at(k, 2)), buf(relay2_in, k), s_send.at[48 + k], s_recv.at[48 + k],
             near(s_axes(k)[1], sign(k)))

    def h2_direct(k):
        send(s_chunk(k, 0, v_at(k, -sign(k))), buf(minus2_in, k), s_send.at[52 + k],
             s_recv.at[52 + k], near(s_axes(k)[1], -sign(k)))

    def h2_relay(k):
        ref = s_chunk(k, 0, v_at(k, sign(k)))
        landed(buf(relay2_in, k), s_send.at[48 + k], s_recv.at[48 + k])
        add_into(ref, buf(relay2_in, k))
        send(ref, buf(plus2_in, k), s_send.at[56 + k], s_recv.at[56 + k],
             near(s_axes(k)[1], sign(k)))

    def h2_sum(k):
        landed(buf(plus2_in, k), s_send.at[56 + k], s_recv.at[56 + k])
        landed(buf(minus2_in, k), s_send.at[52 + k], s_recv.at[52 + k])
        v = s_chunk(k, 0, v_at(k, 0))[...] + buf(plus2_in, k)[...] + buf(minus2_in, k)[...]
        st = k // 2
        final[pl.ds(st * stage_rows[0] + (k % 2) * half[st], half[st]), :] = v

    order = ((0, 2), (1, 2), (0, 1), (0, -1), (1, 1), (1, -1), (0, 0), (1, 0))

    late = []
    for cls, dy in order:
        due, late = late, []
        for st in (0, 1):
            partial_pair(st, cls, dy)
            for dx in (2, 0) if cls == 0 else (1, -1):
                for k in (2 * st, 2 * st + 1):
                    du, j = (dy, v_at(k, dx)) if k % 2 == 0 else (dx, v_at(k, dy))
                    if du == 2:
                        h_far(k, j)
                    elif du == -sign(k):
                        h_direct(k, j)
                    elif du == sign(k):
                        late.append((k, j))
        for k, j in due:
            h_relay(k, j)
    for k, j in late:
        h_relay(k, j)

    for i in range(pts // blk):
        at = pl.ds(i * blk, blk)
        n_line[0:1, at] = zacc[at, :].T[0:1, :]
    n_copy = pltpu.make_async_copy(n_line, n_out, in_sem.at[5])
    n_copy.start()
    for k in quarters:
        h_sum(k, 2)
        h2_far(k)
    for k in quarters:
        h_sum(k, -sign(k))
        h2_direct(k)
    for k in quarters:
        h_sum(k, sign(k))
        h2_relay(k)
    for k in quarters:
        h_sum(k, 0)
    for k in quarters:
        h2_sum(k)

    def block(d):
        return final.at[pl.ds((d % 2) * stage_rows[0] + (d // 2) * blk, blk)]

    def mid_copy(d):
        return remote(
            block(d), mid.at[d - 1], m_send.at[d - 1], m_recv.at[d - 1], (m, partner(s, d))
        )

    def back_source(e):
        if e == 0:
            return block(0)
        if e < NB // 2:
            return flipped.at[e]
        return mid.at[NB - 1 - e]

    def back_copy(e):
        to = back_to(e)
        return remote(back_source(e), back.at[m], d_send.at[e], d_recv.at[m], (to, s))

    def back_to(e):
        if e < NB // 2:
            return partner(s, e)
        d = NB - e
        return md(s - d - NB // 2 * (d % 2), NB)

    def back_put(e):
        to = back_to(e)

        @pl.when(to != m)
        def _():
            back_copy(e).start()

        @pl.when(to == m)
        def _():
            back[m] = back_source(e)[...]

    for d in range(1, NOWN):
        mid_copy(d).start()
    for e in range(NB // 2):
        if e:
            flipped[e] = block(e)[...].astype(F32).T.astype(BF16)
        back_put(e)
    for d in range(1, NOWN):
        landed(mid.at[d - 1], m_send.at[d - 1], m_recv.at[d - 1])
        back_put(NB - d)

    def h_copy(c):
        return pltpu.make_async_copy(masked.at[c], h_out.at[c], out_sem.at[c])

    for k in range(1, NB):
        first_copy(k).wait_send()

    @pl.when(jnp.logical_not(own))
    def _():
        first_copy(0).wait_send()

    for cp in sends:
        cp.wait_send()
    for d in range(1, NOWN):
        mid_copy(d).wait_send()

    for k in (15, 1, 14, 2, 13, 3, 12, 4, 11, 5, 10, 6, 9, 7, 8, 0):
        c = lax.rem(m + k, NB)
        if k:
            landed(back.at[c], d_send.at[0], d_recv.at[c])
        masked[c] = (back[c].astype(F32) * pattern[c, s, m].astype(F32)).astype(BF16)
        h_copy(c).start()

    for e in range(NB):

        @pl.when(back_to(e) != m)
        def _():
            back_copy(e).wait_send()

    n_copy.wait()
    for c in range(NB):
        h_copy(c).wait()


def _widen(h_low, n_row, h_out, n_out):
    h_out[...] = h_low[...].astype(F32)
    n_out[...] = n_row[...]


def body(dens, basis, kern, pert, weight, count, active, pattern):
    blk = dens.shape[1]
    pts = basis.shape[1]
    nact = basis.shape[2] // blk
    rows0, rows1 = (n * blk for n in STAGE_BLOCKS)
    half0 = STAGE_BLOCKS[0] * blk // 2
    vmem = pl.BlockSpec(memory_space=pltpu.VMEM)
    smem = pl.BlockSpec(memory_space=pltpu.SMEM)
    dma = pltpu.SemaphoreType.DMA
    anywhere = pl.BlockSpec(memory_space=pl.ANY)
    h_low, n_row = pl.pallas_call(
        _kernel,
        out_shape=(
            jax.ShapeDtypeStruct((NB, blk, blk), BF16),
            jax.ShapeDtypeStruct((1, pts), F32),
        ),
        in_specs=[anywhere] * 5 + [smem, smem, anywhere],
        out_specs=(anywhere, anywhere),
        scratch_shapes=[
            pltpu.VMEM((NB, blk, blk), BF16),
            pltpu.VMEM((3, 1, pts), F32),
            pltpu.SMEM(pattern.shape, jnp.int32),
            pltpu.VMEM((NB, blk, blk), BF16),
            pltpu.VMEM((nact, pts, blk), BF16),
            pltpu.VMEM((pts, 2 * HALF_EXT * blk), BF16),
            pltpu.VMEM((2 * HALF_EXT * blk, pts), BF16),
            pltpu.VMEM((NB, rows0, blk), BF16),
            pltpu.VMEM((NB, rows1, blk), BF16),
            pltpu.VMEM((pts, blk), F32),
            pltpu.VMEM((pts, blk), F32),
            pltpu.VMEM((3, pts, blk), F32),
            pltpu.VMEM((pts, 2 * blk), BF16),
            pltpu.VMEM((NB, rows0, blk), BF16),
            pltpu.VMEM((NB, rows1, blk), BF16),
            pltpu.VMEM((4, SIDE, half0, blk), BF16),
            pltpu.VMEM((4, SIDE, half0, blk), BF16),
            pltpu.VMEM((4, SIDE, half0, blk), BF16),
            pltpu.VMEM((4, half0, blk), BF16),
            pltpu.VMEM((4, half0, blk), BF16),
            pltpu.VMEM((4, half0, blk), BF16),
            pltpu.VMEM((NOWN * blk, blk), BF16),
            pltpu.VMEM((NB // 2, blk, blk), BF16),
            pltpu.VMEM((NB // 2, blk, blk), BF16),
            pltpu.VMEM((NB, blk, blk), BF16),
            pltpu.VMEM((NB, blk, blk), BF16),
            pltpu.VMEM((1, pts), F32),
            dma((nact,)), dma((6,)), dma((16,)), dma((16,)), dma((64,)), dma((64,)),
            dma((60,)), dma((60,)), dma((8,)), dma((8,)), dma((16,)), dma((16,)), dma((16,)),
        ],
        compiler_params=pltpu.CompilerParams(
            collective_id=0, has_side_effects=True, vmem_limit_bytes=60 * 1024 * 1024
        ),
    )(
        dens, basis.reshape(basis.shape[1:]), kern, pert, weight, count,
        active.reshape(1, active.shape[-1]), pattern,
    )
    return pl.pallas_call(
        _widen,
        out_shape=(
            jax.ShapeDtypeStruct(h_low.shape, F32),
            jax.ShapeDtypeStruct(n_row.shape, F32),
        ),
        in_specs=[vmem, vmem],
        out_specs=(vmem, vmem),
    )(h_low, n_row)


def solution(mesh):
    placed = (
        P(None, "pts", "mat"),
        P("mat", "pts", None),
        P("mat", "pts"),
        P("mat", "pts"),
        P("mat", "pts"),
        P("mat", "pts"),
        P("mat", "pts", None),
        P(),
    )
    return jax.shard_map(
        body,
        mesh=mesh,
        in_specs=placed,
        out_specs=(P(None, "pts", "mat"), P("mat", "pts")),
        check_vma=False,
    )
```
